256 devices in a mesh: tile: 32 (over x, y, core), cuts: 8 (over z).
Axes of the slice: x: 4, y: 4, z: 8, core: 2. Of those that a mesh axis runs over, the one named last changes fastest.
Arguments:
- object_real: float32 [16, 4096, 2048], P('cuts', 'tile'), may hold values from 0.8 to 1.1
- object_imag: float32 [16, 4096, 2048], P('cuts', 'tile'), may hold values from -1.5 to 1.5
- probe: float32 [2, 128, 128], replicated, may hold values from -6 to 6
- positions: int32 [128, 2], P('tile'), may hold values from 0 to 4095, as said below
- counts: int32 [128, 128, 128], P('tile'), may hold values from 0 to 3
Outputs:
- grad_real: float32 [16, 4096, 2048], P('cuts', 'tile')
- grad_imag: float32 [16, 4096, 2048], P('cuts', 'tile')
The draws below stay inside these ranges and needn't reach their ends.
Inputs may be any that keep to these rules, and one draw needn't show every extreme that they name: `positions`: position k has its row within 128 * (k // 4) to 128 * (k // 4) + 127 and its column within 0 to 1920.
All inputs are finite; a program needn't handle non-finite values.
Results may differ from the reference program's by a relative error of at most 0.0003.
Values sent between devices are 32-bit elements; how exact they have to be, the bound alone decides.
A program may use at most 128 MiB of HBM per device.

```python
import math
import jax
import jax.numpy as jnp
from jax import lax

PROBE = 128
TROWS = 128
COLS = 2048
POS_DEV = 4
SLICES = 16
NY = 4096
POS = 128


def draw_positions(key, part):
    key = jax.random.fold_in(key, 11)
    row_key, col_key = jax.random.split(key)
    slot_index = jnp.arange(POS, dtype=jnp.int32)
    strip_index = slot_index // POS_DEV
    leading = slot_index % POS_DEV == 0
    odd_strip = strip_index % 2 == 1
    row_local = jax.random.randint(row_key, (POS,), 0, TROWS, dtype=jnp.int32)
    row_local = jnp.where(leading, jnp.where(odd_strip, TROWS - 1, 0), row_local)
    column = jax.random.randint(col_key, (POS,), 0, COLS - PROBE + 1, dtype=jnp.int32)
    column = jnp.where(leading, jnp.where(odd_strip, 0, COLS - PROBE), column)
    return jnp.stack([strip_index * TROWS + row_local, column], 1).astype(jnp.int32)


def place_ends(drawn, key, smallest, largest):
    spot = [jax.random.randint(jax.random.fold_in(key, axis), (), 0, length) for axis, length in enumerate(drawn.shape)]
    main_axis = drawn.shape.index(max(drawn.shape))
    beside = spot[:main_axis] + [(spot[main_axis] + 1) % drawn.shape[main_axis]] + spot[main_axis + 1:]
    return drawn.at[tuple(spot)].set(smallest).at[tuple(beside)].set(largest)


def steps_of(rng, extent, pieces, smallest, largest):
    def one(dim, blocks):
        draws = jax.random.uniform(jax.random.fold_in(jax.random.fold_in(rng, 6), dim), (blocks,), jnp.float32, smallest / len(pieces), largest / len(pieces))
        return jnp.repeat(jnp.exp(draws), extent[dim] // blocks).reshape((-1,) + (1,) * (len(extent) - dim - 1))

    factor_of = one(*pieces[0])
    for cut in pieces[1:]:
        factor_of = factor_of * one(*cut)
    return factor_of


def bell_draw(rng, shape, spread, bound, cuts=(), kind=jnp.bfloat16):
    result = spread * jax.random.normal(rng, shape, jnp.float32)
    if cuts:
        result = result * steps_of(rng, shape, cuts, -0.22, 0.18)
    return jnp.clip(result, -bound, bound).astype(kind)


def setup_inputs(seed: int = 0) -> dict:
    key_list = jax.random.split(jax.random.key(seed), 6)
    return {
        "object_real": jnp.clip(0.8 + 0.3 * jax.random.uniform(key_list[0], (SLICES, NY, COLS), jnp.float32) ** steps_of(key_list[0], (SLICES, NY, COLS), ((0, 8), (1, 32)), -0.2, 0.2), 0.8, 1.1),
        "object_imag": bell_draw(key_list[1], (SLICES, NY, COLS), 0.25, 1.5, ((0, 8), (1, 32)), jnp.float32),
        "probe": bell_draw(key_list[2], (2, PROBE, PROBE), 1.0, 6.0, (), jnp.float32),
        "positions": draw_positions(jax.random.fold_in(key_list[5], 71), 0),
        "counts": place_ends(jax.random.randint(key_list[4], (POS, PROBE, PROBE), 0, 4), jax.random.fold_in(key_list[4], 1), 0, 3).astype(jnp.int32),
    }


phase_scale = 32.0

def dft_tables(window):
    index_int = jnp.arange(window, dtype=jnp.int32)
    product = index_int[:, None] * index_int[None, :] % window
    angle = 2.0 * math.pi / window * product.astype(jnp.float32)
    norm_factor = 1.0 / math.sqrt(window)
    cos_table = jnp.cos(angle) * norm_factor
    sin_table = -jnp.sin(angle) * norm_factor
    freq = jnp.where(index_int < window // 2, index_int, index_int - window).astype(jnp.float32)
    chirp = phase_scale * (freq[:, None] ** 2 + freq[None, :] ** 2) / (window * window)
    return (cos_table, sin_table, jnp.cos(chirp), -jnp.sin(chirp))

def left_times(matrix, field):
    return jnp.einsum('jk,...kl->...jl', matrix, field, precision=lax.Precision.HIGHEST)

def right_times(field, matrix):
    return jnp.einsum('...jk,kl->...jl', field, matrix, precision=lax.Precision.HIGHEST)

def transform(real_part, imag_part, cos_table, sin_table, sign):
    sin_signed = sign * sin_table
    left_re = left_times(cos_table, real_part) - left_times(sin_signed, imag_part)
    left_im = left_times(cos_table, imag_part) + left_times(sin_signed, real_part)
    out_re = right_times(left_re, cos_table) - right_times(left_im, sin_signed)
    out_im = right_times(left_re, sin_signed) + right_times(left_im, cos_table)
    return (out_re, out_im)

def propagate(real_part, imag_part, tables, sign):
    cos_table, sin_table, phase_re, phase_im = tables
    freq_re, freq_im = transform(real_part, imag_part, cos_table, sin_table, 1.0)
    turned_re = phase_re * freq_re - sign * phase_im * freq_im
    turned_im = phase_re * freq_im + sign * phase_im * freq_re
    return transform(turned_re, turned_im, cos_table, sin_table, -1.0)

def reference(object_real, object_imag, probe, positions, counts):
    tables = dft_tables(PROBE)
    cos_table, sin_table = (tables[0], tables[1])
    offsets = jnp.arange(PROBE, dtype=jnp.int32)

    def one_position(grads, inputs):
        place, measured = inputs
        row_index = (place[0] + offsets) % NY
        col_index = place[1] + offsets
        patch_re = lax.dynamic_slice_in_dim(object_real[:, row_index, :], place[1], PROBE, 2)
        patch_im = lax.dynamic_slice_in_dim(object_imag[:, row_index, :], place[1], PROBE, 2)
        wave_re, wave_im = (probe[0], probe[1])
        kept = []
        for layer in range(SLICES):
            kept.append((wave_re, wave_im))
            mixed_re = patch_re[layer] * wave_re - patch_im[layer] * wave_im
            mixed_im = patch_re[layer] * wave_im + patch_im[layer] * wave_re
            wave_re, wave_im = propagate(mixed_re, mixed_im, tables, 1.0)
        far_re, far_im = transform(wave_re, wave_im, cos_table, sin_table, 1.0)
        weight = 4.0 * (far_re * far_re + far_im * far_im - measured.astype(jnp.float32))
        grad_re, grad_im = transform(weight * far_re, weight * far_im, cos_table, sin_table, -1.0)
        pieces_re = [None] * SLICES
        pieces_im = [None] * SLICES
        for layer in range(SLICES - 1, -1, -1):
            back_re, back_im = propagate(grad_re, grad_im, tables, -1.0)
            kept_re, kept_im = kept[layer]
            pieces_re[layer] = kept_re * back_re + kept_im * back_im
            pieces_im[layer] = kept_re * back_im - kept_im * back_re
            grad_re = patch_re[layer] * back_re + patch_im[layer] * back_im
            grad_im = patch_re[layer] * back_im - patch_im[layer] * back_re
        total_re, total_im = grads
        total_re = total_re.at[:, row_index[:, None], col_index[None, :]].add(jnp.stack(pieces_re, 0))
        total_im = total_im.at[:, row_index[:, None], col_index[None, :]].add(jnp.stack(pieces_im, 0))
        return ((total_re, total_im), None)
    start = (jnp.zeros_like(object_real), jnp.zeros_like(object_imag))
    (grad_real, grad_imag), unused = lax.scan(one_position, start, (positions, counts))
    return (grad_real, grad_imag)
```

```python
import functools
import math

import jax
import jax.numpy as jnp
import ml_dtypes
import numpy as np
from jax import lax
from jax.experimental import pallas as pl
from jax.experimental.pallas import tpu as pltpu
from jax.sharding import PartitionSpec as P

f32, bf16 = jnp.float32, jnp.bfloat16
phase_scale = 32.0
TILE, CUTS = "tile", "cuts"
RIGHT_A, RIGHT_A_CONJ, RIGHT_F, RIGHT_F_CONJ = range(4)


def tables(n):
    index = np.arange(n)
    dft = np.exp(-2j * np.pi * (np.outer(index, index) % n) / n) / math.sqrt(n)
    freq = np.where(index < n // 2, index, index - n).astype(np.float64)
    turn = np.exp(-1j * phase_scale * freq**2 / (n * n))
    step = np.conj(dft) @ (turn[:, None] * dft)

    def parts(matrix):
        block = np.block([[matrix.real, matrix.imag], [-matrix.imag, matrix.real]])
        high = block.astype(ml_dtypes.bfloat16)
        low = (block - high.astype(np.float64)).astype(ml_dtypes.bfloat16)
        rest = (block - high.astype(np.float64) - low.astype(np.float64)).astype(ml_dtypes.bfloat16)
        return high, low, rest

    rights, lefts = [], []
    for matrix in (step, step.conj(), dft, dft.conj()):
        high, low, rest = parts(matrix)
        rights.append(np.concatenate([high, high, low, rest], 0))
        lefts.append(np.concatenate([high.T, low.T, rest.T], 1))
    return np.stack(rights), np.stack(lefts)


def split(value):
    high = value.astype(bf16)
    return high, (value - high.astype(f32)).astype(bf16)


def dot(a, b):
    return jnp.dot(a, b, preferred_element_type=f32)


def right_times(re, im, table):
    n = re.shape[1]
    high, low = split(jnp.concatenate([re, im], 1))
    out = dot(jnp.concatenate([high, low, high, high], 1), table[...])
    return out[:, :n], out[:, n:]


def left_times(re, im, table):
    n = re.shape[0]
    high, low = split(jnp.concatenate([re, im], 0))
    main = dot(table[:, : 2 * n], jnp.concatenate([high, low], 1))
    rest = dot(table[:, 2 * n :], jnp.concatenate([high, high], 0))
    out = main[:, :n] + main[:, n:] + rest
    return out[:n], out[n:]


def both_sides(re, im, rights, lefts, which):
    re, im = right_times(re, im, rights.at[which])
    return left_times(re, im, lefts.at[which])


def wave_kernel(patch_at, probe, counts, rights, lefts, out, psi):
    count = psi.shape[0]

    psi[0] = probe[...]

    def forward(s, carry):
        a, b = psi[s, 0], psi[s, 1]
        p, q = patch_at(s)
        re, im = both_sides(p * a - q * b, p * b + q * a, rights, lefts, RIGHT_A)
        psi[s + 1, 0] = re
        psi[s + 1, 1] = im
        return carry

    lax.fori_loop(0, count - 1, forward, 0)
    a, b = psi[count - 1, 0], psi[count - 1, 1]
    p, q = patch_at(count - 1)
    re, im = both_sides(p * a - q * b, p * b + q * a, rights, lefts, RIGHT_F)
    weight = 4.0 * (re * re + im * im - counts.astype(f32))
    re, im = both_sides(weight * re, weight * im, rights, lefts, RIGHT_F_CONJ)

    def put(s, re, im):
        a, b = psi[s, 0], psi[s, 1]
        out[s, 0] = a * re + b * im
        out[s, 1] = a * im - b * re

    put(count - 1, re, im)

    def backward(i, carry):
        re, im = carry
        s = count - 1 - i
        p, q = patch_at(s)
        re, im = both_sides(p * re + q * im, p * im - q * re, rights, lefts, RIGHT_A_CONJ)
        put(s - 1, re, im)
        return re, im

    lax.fori_loop(0, count - 1, backward, (re, im))


def take_kernel(meta, real0, real1, imag0, imag1, probe, win, rolled):
    w = pl.program_id(0)
    n = probe.shape[1]
    shape = (n, n)
    rows = lax.broadcasted_iota(jnp.int32, shape, 0)
    cols = lax.broadcasted_iota(jnp.int32, shape, 1)
    split_row, split_col = meta[1, w], meta[2, w]
    own = w < pl.num_programs(0) // 2
    keep = jnp.where(own, (rows >= split_row).astype(jnp.int32), (rows < split_row).astype(jnp.int32)) > 0
    first = cols >= split_col
    for s in range(real0.shape[0]):
        win[0, s, 0] = jnp.where(keep, jnp.where(first, real0[s], real1[s]), 0.0)
        win[0, s, 1] = jnp.where(keep, jnp.where(first, imag0[s], imag1[s]), 0.0)

    @pl.when(w == 0)
    def _():
        at = meta.shape[1] - 1
        for i in range(2):
            turned = pltpu.roll(probe[i], meta[1, at], 0)
            rolled[i] = pltpu.roll(turned, meta[2, at], 1)


def take(meta, object_real, object_imag, probe):
    slices, rows, cols = object_real.shape
    n = probe.shape[1]
    count = meta.shape[1] - 1
    last = cols // n - 1
    block = lambda index: pl.BlockSpec((slices, n, n), index)
    here = lambda w, meta: (0, 0, meta[0, w])
    beside = lambda w, meta: (0, 0, jnp.minimum(meta[0, w] + 1, last))
    return pl.pallas_call(
        take_kernel,
        out_shape=(
            jax.ShapeDtypeStruct((count, slices, 2, n, n), f32),
            jax.ShapeDtypeStruct((2, n, n), f32),
        ),
        grid_spec=pltpu.PrefetchScalarGridSpec(
            num_scalar_prefetch=1,
            grid=(count,),
            in_specs=[
                block(here),
                block(beside),
                block(here),
                block(beside),
                pl.BlockSpec((2, n, n), lambda w, meta: (0, 0, 0)),
            ],
            out_specs=(
                pl.BlockSpec((1, slices, 2, n, n), lambda w, meta: (w, 0, 0, 0, 0)),
                pl.BlockSpec((2, n, n), lambda w, meta: (0, 0, 0)),
            ),
        ),
    )(meta, object_real, object_real, object_imag, object_imag, probe)


def add_kernel(meta, own, other, real, imag):
    n = own.shape[-1]
    count = own.shape[0]
    shape = (n, n)
    rows = lax.broadcasted_iota(jnp.int32, shape, 0)
    cols = lax.broadcasted_iota(jnp.int32, shape, 1)
    last = real.shape[2] // n - 1
    real[...] = jnp.zeros_like(real)
    imag[...] = jnp.zeros_like(imag)
    for w in range(2 * count):
        source = own.at[w] if w < count else other.at[w - count]
        block, split_row, split_col = meta[0, w], meta[1, w], meta[2, w]
        keep = (rows >= split_row) if w < count else (rows < split_row)
        here = pl.ds(pl.multiple_of(block * n, n), n)
        beside = pl.ds(pl.multiple_of(jnp.minimum(block + 1, last) * n, n), n)
        first = cols >= split_col
        for i, target in enumerate((real, imag)):
            value = jnp.where(keep, source[0, i], 0.0)
            target[0, :, here] += jnp.where(first, value, 0.0)
            target[0, :, beside] += jnp.where(first, 0.0, value)


def add(meta, own, other, shape):
    slices, rows, cols = shape
    count, _, _, n, _ = own.shape
    window = pl.BlockSpec((count, 1, 2, n, n), lambda s, meta: (0, s, 0, 0, 0))
    strip = pl.BlockSpec((1, rows, cols), lambda s, meta: (s, 0, 0))
    return pl.pallas_call(
        add_kernel,
        out_shape=(jax.ShapeDtypeStruct(shape, f32),) * 2,
        grid_spec=pltpu.PrefetchScalarGridSpec(
            num_scalar_prefetch=1,
            grid=(slices,),
            in_specs=[window, window],
            out_specs=(strip, strip),
        ),
        compiler_params=pltpu.CompilerParams(vmem_limit_bytes=32 << 20),
    )(meta, own, other)


def plain_kernel(patches, probe, counts, rights, lefts, out, psi):
    me = lax.axis_index(CUTS)
    cuts, slices = patches.shape[:2]

    def patch_at(s):
        at, inner = lax.rem(me - s // slices + cuts, cuts), lax.rem(s, slices)
        return patches[at, inner, 0], patches[at, inner, 1]

    wave_kernel(patch_at, probe, counts[...], rights, lefts, out, psi)


def shards(object_real, object_imag, probe, positions, counts):
    cuts, tiles = lax.axis_size(CUTS), lax.axis_size(TILE)
    me, tile = lax.axis_index(CUTS), lax.axis_index(TILE)
    slices, rows, cols = object_real.shape
    n = probe.shape[1]
    count = positions.shape[0]
    spread = cuts // count
    phase = lax.rem(tile, spread)
    back = [(t, (t - 1) % tiles) for t in range(tiles)]
    ahead = [(t, (t + 1) % tiles) for t in range(tiles)]

    def places(position):
        return jnp.stack([position[:, 1] // n, position[:, 0] % n, position[:, 1] % n])

    own_places = places(positions)
    other_places = lax.ppermute(own_places, TILE, ahead)
    held = lax.div(me + cuts - phase, spread) % count
    mine = lax.dynamic_slice_in_dim(own_places, held, 1, 1)
    meta = jnp.concatenate([own_places, other_places, mine], 1)
    windows, rolled = take(meta, object_real, object_imag, probe)
    merged = windows[:count] + lax.ppermute(windows[count:], TILE, back)

    def owner(k, t):
        return (k * spread + t % spread) % cuts

    def pairs(d):
        out = []
        for t in range(tiles):
            for k in range(count):
                o = owner(k, t)
                out.append((t * cuts + (o - d) % cuts, t * cuts + o))
        return out

    got = []
    for d in range(cuts):
        k = lax.div(lax.rem(me + d + cuts - phase, cuts), spread)
        piece = lax.dynamic_index_in_dim(merged, k, 0, False)
        got.append(piece if d == 0 else lax.ppermute(piece, (TILE, CUTS), pairs(d)))
    patches = jnp.stack(got)
    rights, lefts = (jnp.asarray(t) for t in tables(n))
    contrib = pl.pallas_call(
        plain_kernel,
        out_shape=jax.ShapeDtypeStruct((cuts * slices, 2, n, n), f32),
        in_specs=[pl.BlockSpec(memory_space=pltpu.VMEM)] * 5,
        out_specs=pl.BlockSpec(memory_space=pltpu.VMEM),
        scratch_shapes=[pltpu.VMEM((cuts * slices, 2, n, n), f32)],
        compiler_params=pltpu.CompilerParams(vmem_limit_bytes=40 << 20),
    )(patches, rolled, lax.dynamic_index_in_dim(counts, held, 0, False), rights, lefts)
    contrib = contrib.reshape(cuts, slices, 2, n, n)
    is_owner = lax.rem(me + cuts - phase, spread) == 0
    sums = [0.0] * count
    for d in range(cuts):
        piece = lax.dynamic_index_in_dim(contrib, lax.rem(me - d + cuts, cuts), 0, False)
        if d == 0:
            piece = jnp.where(is_owner, piece, 0.0)
        else:
            piece = lax.ppermute(piece, (TILE, CUTS), [(b, a) for a, b in pairs(d)])
        sums[d // spread] = sums[d // spread] + piece
    own = jnp.stack(sums)
    order = []
    lag = lax.rem(phase - me + cuts, spread)
    for j in range(count):
        o = lax.rem(me + j * spread + lag, cuts)
        order.append(lax.div(lax.rem(o - phase + cuts, cuts), spread))
    picked = own_places[:, jnp.stack(order)]
    other = lax.ppermute(own, TILE, ahead)
    meta = jnp.concatenate([picked, lax.ppermute(picked, TILE, ahead)], 1)
    return add(meta, own, other, object_real.shape)


def solution(mesh):
    placed = (
        P("cuts", "tile", None),
        P("cuts", "tile", None),
        P(),
        P("tile", None),
        P("tile", None, None),
    )
    return jax.shard_map(
        shards,
        mesh=mesh,
        in_specs=placed,
        out_specs=(P("cuts", "tile", None), P("cuts", "tile", None)),
        check_vma=False,
    )
```

```python
import functools
import math

import jax
import jax.numpy as jnp
import ml_dtypes
import numpy as np
from jax import lax
from jax.experimental import pallas as pl
from jax.experimental.pallas import tpu as pltpu
from jax.sharding import PartitionSpec as P

f32, bf16 = jnp.float32, jnp.bfloat16
phase_scale = 32.0
TILE, CUTS = "tile", "cuts"
RIGHT_A, RIGHT_A_CONJ, RIGHT_F, RIGHT_F_CONJ = range(4)


def tables(n):
    index = np.arange(n)
    dft = np.exp(-2j * np.pi * (np.outer(index, index) % n) / n) / math.sqrt(n)
    freq = np.where(index < n // 2, index, index - n).astype(np.float64)
    turn = np.exp(-1j * phase_scale * freq**2 / (n * n))
    step = np.conj(dft) @ (turn[:, None] * dft)

    def parts(matrix):
        block = np.block([[matrix.real, matrix.imag], [-matrix.imag, matrix.real]])
        high = block.astype(ml_dtypes.bfloat16)
        low = (block - high.astype(np.float64)).astype(ml_dtypes.bfloat16)
        rest = (block - high.astype(np.float64) - low.astype(np.float64)).astype(ml_dtypes.bfloat16)
        return high, low, rest

    rights, lefts = [], []
    for matrix in (step, step.conj(), dft, dft.conj()):
        high, low, rest = parts(matrix)
        rights.append(np.concatenate([high, low, rest], 0))
        lefts.append(np.concatenate([high.T, low.T, rest.T], 1))
    return np.stack(rights), np.stack(lefts)


def split(value):
    high = value.astype(bf16)
    return high, (value - high.astype(f32)).astype(bf16)


def dot(a, b):
    return jnp.dot(a, b, preferred_element_type=f32)


def right_times(re, im, table):
    n = re.shape[1]
    high, low = split(jnp.concatenate([re, im], 1))
    parts = jnp.concatenate([table[: 2 * n], table[...]], 0)
    out = dot(jnp.concatenate([low, high, high, high], 1), parts)
    return out[:, :n], out[:, n:]


def left_times(re, im, table):
    n = re.shape[0]
    high, low = split(jnp.concatenate([re, im], 0))
    main = dot(table[:, : 2 * n], jnp.concatenate([high, low], 1))
    rest = dot(table[:, 2 * n :], jnp.concatenate([high, high], 0))
    out = main[:, :n] + main[:, n:] + rest
    return out[:n], out[n:]


def both_sides(re, im, rights, lefts, which):
    re, im = right_times(re, im, rights.at[which])
    return left_times(re, im, lefts.at[which])


def fused_kernel(
    places,
    places_before,
    probe,
    counts,
    real_hbm,
    imag_hbm,
    rights_hbm,
    lefts_hbm,
    own_out,
    other_out,
    real,
    imag,
    rights,
    lefts,
    rim_out,
    rim_in,
    merged,
    patches,
    psi,
    contrib,
    load_sem,
    table_sem,
    rim_send,
    rim_recv,
    gather_send,
    gather_recv,
    back_send,
    back_recv,
    ahead_send,
    ahead_recv,
):
    cuts, tiles = lax.axis_size(CUTS), lax.axis_size(TILE)
    me, tile = lax.axis_index(CUTS), lax.axis_index(TILE)
    above = lax.rem(tile + tiles - 1, tiles)
    below = lax.rem(tile + 1, tiles)
    slices, rows, cols = real.shape
    n = probe.shape[1]
    count = merged.shape[0]
    total = cuts * slices
    spread = cuts // count
    phase = lax.rem(tile, spread)
    mine = lax.div(lax.rem(me - phase + cuts, cuts), spread)

    def device(t, z):
        return dict(device_id=(t, z), device_id_type=pl.DeviceIdType.MESH)

    loads = []
    for i, (source, target) in enumerate(((real_hbm, real), (imag_hbm, imag))):
        for s in range(slices):
            loads.append(pltpu.make_async_copy(source.at[s], target.at[s], load_sem.at[i, s]))
    table_loads = [
        pltpu.make_async_copy(rights_hbm, rights, table_sem.at[0]),
        pltpu.make_async_copy(lefts_hbm, lefts, table_sem.at[1]),
    ]
    for copy in loads + table_loads:
        copy.start()

    barrier = pltpu.get_barrier_semaphore()
    for d in range(1, cuts):
        pl.semaphore_signal(barrier, inc=1, **device(tile, lax.rem(me + d, cuts)))
    pl.semaphore_signal(barrier, inc=1, **device(above, me))
    pl.semaphore_signal(barrier, inc=1, **device(below, me))

    row_at = lax.broadcasted_iota(jnp.int32, (n, n), 0)
    col_at = lax.broadcasted_iota(jnp.int32, (n, n), 1)

    def window(where, k, target, own):
        row = lax.rem(where[k, 0], n)
        column = where[k, 1]
        block = lax.div(column, n)
        keep = row_at >= row if own else row_at < row
        wanted = jnp.where(col_at >= column - block * n, block, block + 1)
        for s in range(slices):
            for i, source in enumerate((real, imag)):
                value = jnp.zeros((n, n), f32)
                for at in range(cols // n):
                    value = jnp.where(wanted == at, source[s, :, at * n : (at + 1) * n], value)
                target[k, s, i] = jnp.where(keep, value, 0.0)

    def turn(j):
        return lax.rem(lax.div(me, spread) + j, count)

    def rim_copy(k):
        return pltpu.make_async_remote_copy(
            rim_out.at[k], rim_in.at[k], rim_send.at[k], rim_recv.at[k], **device(above, me)
        )

    def owner(k):
        return lax.rem(k * spread + phase, cuts)

    def gather_copy(k):
        return pltpu.make_async_remote_copy(
            merged.at[k], patches.at[me], gather_send.at[k], gather_recv.at[me], **device(tile, owner(k))
        )

    def arrival(z):
        return pltpu.make_async_remote_copy(
            merged.at[0], patches.at[z], gather_send.at[0], gather_recv.at[z], **device(tile, z)
        )

    for copy in loads:
        copy.wait()
    pl.semaphore_wait(barrier, cuts + 1)

    def send_rim(j, carry):
        k = turn(j)
        window(places_before, k, rim_out, False)
        rim_copy(k).start()
        return carry

    lax.fori_loop(0, count, send_rim, 0)

    def take_own(j, carry):
        window(places, turn(j), merged, True)
        return carry

    lax.fori_loop(0, count, take_own, 0)

    def send_windows(j, carry):
        k = turn(j)
        rim_copy(k).wait_recv()
        for s in range(slices):
            for i in range(2):
                merged[k, s, i] = merged[k, s, i] + rim_in[k, s, i]

        @pl.when(owner(k) != me)
        def _():
            gather_copy(k).start()

        @pl.when(owner(k) == me)
        def _():
            for s in range(slices):
                for i in range(2):
                    patches[me, s, i] = merged[k, s, i]

        return carry

    lax.fori_loop(0, count, send_windows, 0)
    for copy in table_loads:
        copy.wait()

    def back_copy(s):
        inner = lax.rem(s, slices)
        return pltpu.make_async_remote_copy(
            contrib.at[s],
            own_out.at[mine, inner],
            back_send.at[s],
            back_recv.at[mine, inner],
            **device(tile, lax.div(s, slices)),
        )

    def keep_copy(s):
        return pltpu.make_async_copy(
            contrib.at[s], own_out.at[mine, lax.rem(s, slices)], back_send.at[s]
        )

    def put(s, re, im):
        a, b = psi[s, 0], psi[s, 1]
        contrib[s, 0] = a * re + b * im
        contrib[s, 1] = a * im - b * re
        z = lax.div(s, slices)

        @pl.when(z != me)
        def _():
            back_copy(s).start()

        @pl.when(z == me)
        def _():
            keep_copy(s).start()

    def patch_at(s):
        z, inner = lax.div(s, slices), lax.rem(s, slices)
        return patches[z, inner, 0], patches[z, inner, 1]

    @pl.when(owner(mine) == me)
    def _():
        row, column = lax.rem(places[mine, 0], n), lax.rem(places[mine, 1], n)
        a, b = probe[0], probe[1]
        bit = 1
        while bit < n:
            for axis, amount in ((0, row), (1, column)):
                take = (jnp.full((n, n), amount, jnp.int32) & bit) > 0
                a = jnp.where(take, pltpu.roll(a, bit, axis), a)
                b = jnp.where(take, pltpu.roll(b, bit, axis), b)
            bit *= 2
        psi[0, 0] = a
        psi[0, 1] = b

        def forward(s, carry):
            z = lax.div(s, slices)

            @pl.when((lax.rem(s, slices) == 0) & (z != me))
            def _():
                arrival(z).wait_recv()

            a, b = psi[s, 0], psi[s, 1]
            p, q = patch_at(s)
            re, im = both_sides(p * a - q * b, p * b + q * a, rights, lefts, RIGHT_A)
            psi[s + 1, 0] = re
            psi[s + 1, 1] = im
            return carry

        lax.fori_loop(0, total - 1, forward, 0)
        a, b = psi[total - 1, 0], psi[total - 1, 1]
        p, q = patch_at(total - 1)
        re, im = both_sides(p * a - q * b, p * b + q * a, rights, lefts, RIGHT_F)
        weight = 4.0 * (re * re + im * im - counts[mine].astype(f32))
        re, im = both_sides(weight * re, weight * im, rights, lefts, RIGHT_F_CONJ)
        put(total - 1, re, im)

        def backward(i, carry):
            re, im = carry
            s = total - 1 - i
            p, q = patch_at(s)
            re, im = both_sides(p * re + q * im, p * im - q * re, rights, lefts, RIGHT_A_CONJ)
            put(s - 1, re, im)
            return re, im

        lax.fori_loop(0, total - 1, backward, (re, im))

    def term_copy(k, s):
        return pltpu.make_async_remote_copy(
            contrib.at[0], own_out.at[k, s], back_send.at[0], back_recv.at[k, s], **device(tile, owner(k))
        )

    def ahead_copy(k, s):
        return pltpu.make_async_remote_copy(
            own_out.at[k, s], other_out.at[k, s], ahead_send.at[k, s], ahead_recv.at[k, s], **device(below, me)
        )

    def pass_on(step, carry):
        s = slices - 1 - lax.div(step, count)
        k = turn(lax.rem(step, count))

        @pl.when(owner(k) != me)
        def _():
            term_copy(k, s).wait_recv()

        @pl.when(owner(k) == me)
        def _():
            keep_copy(me * slices + s).wait()

        ahead_copy(k, s).start()
        return carry

    lax.fori_loop(0, count * slices, pass_on, 0)

    def finish(step, carry):
        s, k = lax.div(step, count), lax.rem(step, count)
        ahead_copy(k, s).wait()
        return carry

    lax.fori_loop(0, count * slices, finish, 0)

    def finish_windows(k, carry):
        rim_copy(k).wait_send()

        @pl.when(owner(k) != me)
        def _():
            gather_copy(k).wait_send()

        return carry

    lax.fori_loop(0, count, finish_windows, 0)

    @pl.when(owner(mine) == me)
    def _():
        def finish_back(s, carry):
            @pl.when(lax.div(s, slices) != me)
            def _():
                back_copy(s).wait_send()

            return carry

        lax.fori_loop(0, total, finish_back, 0)


def add_kernel(places, places_before, own, other, real, imag):
    n = own.shape[-1]
    count = own.shape[0]
    rows = lax.broadcasted_iota(jnp.int32, (n, n), 0)
    cols = lax.broadcasted_iota(jnp.int32, (n, n), 1)
    last = real.shape[2] // n - 1
    real[...] = jnp.zeros_like(real)
    imag[...] = jnp.zeros_like(imag)
    for where, source, is_own in ((places, own, True), (places_before, other, False)):
        for k in range(count):
            row = lax.rem(where[k, 0], n)
            column = where[k, 1]
            block = lax.div(column, n)
            keep = (rows >= row) if is_own else (rows < row)
            here = pl.ds(pl.multiple_of(block * n, n), n)
            beside = pl.ds(pl.multiple_of(jnp.minimum(block + 1, last) * n, n), n)
            first = cols >= column - block * n
            for i, target in enumerate((real, imag)):
                value = jnp.where(keep, source[k, 0, i], 0.0)
                target[0, :, here] += jnp.where(first, value, 0.0)
                target[0, :, beside] += jnp.where(first, 0.0, value)


def add(places, places_before, own, other, shape):
    slices, rows, cols = shape
    count, _, _, n, _ = own.shape
    window = pl.BlockSpec((count, 1, 2, n, n), lambda s, *_: (0, s, 0, 0, 0))
    strip = pl.BlockSpec((1, rows, cols), lambda s, *_: (s, 0, 0))
    return pl.pallas_call(
        add_kernel,
        out_shape=(jax.ShapeDtypeStruct(shape, f32),) * 2,
        grid_spec=pltpu.PrefetchScalarGridSpec(
            num_scalar_prefetch=2,
            grid=(slices,),
            in_specs=[window, window],
            out_specs=(strip, strip),
        ),
        compiler_params=pltpu.CompilerParams(vmem_limit_bytes=32 << 20),
    )(places, places_before, own, other)


def shards(object_real, object_imag, probe, positions, counts):
    cuts, tiles = lax.axis_size(CUTS), lax.axis_size(TILE)
    slices, rows, cols = object_real.shape
    n = probe.shape[1]
    count = positions.shape[0]
    before = lax.ppermute(positions, TILE, [(t, (t + 1) % tiles) for t in range(tiles)])
    rights, lefts = (jnp.asarray(t) for t in tables(n))
    windows = (count, slices, 2, n, n)
    total = cuts * slices
    vmem = pl.BlockSpec(memory_space=pltpu.VMEM)
    smem = pl.BlockSpec(memory_space=pltpu.SMEM)
    hbm = pl.BlockSpec(memory_space=pl.ANY)
    dma = pltpu.SemaphoreType.DMA
    own, other = pl.pallas_call(
        fused_kernel,
        out_shape=(jax.ShapeDtypeStruct(windows, f32),) * 2,
        in_specs=[smem, smem, vmem, vmem, hbm, hbm, hbm, hbm],
        out_specs=(hbm, hbm),
        scratch_shapes=[
            pltpu.VMEM(object_real.shape, f32),
            pltpu.VMEM(object_imag.shape, f32),
            pltpu.VMEM(rights.shape, bf16),
            pltpu.VMEM(lefts.shape, bf16),
            pltpu.VMEM(windows, f32),
            pltpu.VMEM(windows, f32),
            pltpu.VMEM(windows, f32),
            pltpu.VMEM((cuts, slices, 2, n, n), f32),
            pltpu.VMEM((total, 2, n, n), f32),
            pltpu.VMEM((total, 2, n, n), f32),
            dma((2, slices)),
            dma((2,)),
            dma((count,)),
            dma((count,)),
            dma((count,)),
            dma((cuts,)),
            dma((total,)),
            dma((count, slices)),
            dma((count, slices)),
            dma((count, slices)),
        ],
        compiler_params=pltpu.CompilerParams(
            collective_id=0, has_side_effects=True, vmem_limit_bytes=40 << 20
        ),
    )(positions, before, probe, counts, object_real, object_imag, rights, lefts)
    return add(positions, before, own, other, object_real.shape)


def solution(mesh):
    placed = (
        P("cuts", "tile", None),
        P("cuts", "tile", None),
        P(),
        P("tile", None),
        P("tile", None, None),
    )
    return jax.shard_map(
        shards,
        mesh=mesh,
        in_specs=placed,
        out_specs=(P("cuts", "tile", None), P("cuts", "tile", None)),
        check_vma=False,
    )
```

```python
import functools
import math

import jax
import jax.numpy as jnp
import numpy as np
from jax import lax
from jax.experimental import pallas as pl
from jax.experimental.pallas import tpu as pltpu
from jax.sharding import PartitionSpec as P

f32, bf16 = jnp.float32, jnp.bfloat16
phase_scale = 32.0
TILE, CUTS = "tile", "cuts"
RIGHT_A, RIGHT_A_CONJ, RIGHT_F, RIGHT_F_CONJ = range(4)


def tables(n):
    index = np.arange(n)
    dft = np.exp(-2j * np.pi * (np.outer(index, index) % n) / n) / math.sqrt(n)
    freq = np.where(index < n // 2, index, index - n).astype(np.float64)
    turn = np.exp(-1j * phase_scale * freq**2 / (n * n))
    step = np.conj(dft) @ (turn[:, None] * dft)

    out = []
    for matrix in (step, dft):
        block = np.block([[matrix.real, matrix.imag], [-matrix.imag, matrix.real]])
        out += [block, block.T]
    return np.stack(out).astype(np.float32)


def split(value):
    high = value.astype(bf16)
    return high, (value - high.astype(f32)).astype(bf16)


def dot(a, b):
    return jnp.dot(a, b, preferred_element_type=f32)


def right_times(re, im, table):
    n = re.shape[1]
    high, low = split(jnp.concatenate([re, im], 1))
    parts = jnp.concatenate([table[: 2 * n], table[...]], 0)
    out = dot(jnp.concatenate([low, high, high, high], 1), parts)
    return out[:, :n], out[:, n:]


def left_times(re, im, table):
    n = re.shape[0]
    high, low = split(jnp.concatenate([re, im], 0))
    main = dot(table[:, : 2 * n], jnp.concatenate([high, low], 1))
    rest = dot(table[:, 2 * n :], jnp.concatenate([high, high], 0))
    out = main[:, :n] + main[:, n:] + rest
    return out[:n], out[n:]


def both_sides(re, im, rights, lefts, which):
    re, im = right_times(re, im, rights.at[which])
    return left_times(re, im, lefts.at[which])


def fused_kernel(
    places,
    places_before,
    probe_hbm,
    counts_hbm,
    real_hbm,
    imag_hbm,
    blocks_hbm,
    own_out,
    other_out,
    real,
    imag,
    probe,
    counts,
    blocks,
    rights,
    lefts,
    rim_out,
    rim_in,
    merged,
    patches,
    psi,
    contrib,
    load_sem,
    table_sem,
    counts_send,
    counts_recv,
    rim_send,
    rim_recv,
    gather_send,
    gather_recv,
    back_send,
    back_recv,
    ahead_send,
    ahead_recv,
):
    cuts, tiles = lax.axis_size(CUTS), lax.axis_size(TILE)
    me, tile = lax.axis_index(CUTS), lax.axis_index(TILE)
    above = lax.rem(tile + tiles - 1, tiles)
    below = lax.rem(tile + 1, tiles)
    slices, rows, cols = real.shape
    n = probe.shape[1]
    count = merged.shape[0]
    total = cuts * slices
    spread = cuts // count
    phase = lax.rem(tile, spread)
    mine = lax.div(lax.rem(me - phase + cuts, cuts), spread)
    is_owner = lax.rem(me - phase + cuts, spread) == 0
    half = count // 2

    def device(t, z):
        return dict(device_id=(t, z), device_id_type=pl.DeviceIdType.MESH)

    loads = []
    for i, (source, target) in enumerate(((real_hbm, real), (imag_hbm, imag))):
        for s in range(slices):
            loads.append(pltpu.make_async_copy(source.at[s], target.at[s], load_sem.at[i, s]))
    table_loads = [
        pltpu.make_async_copy(blocks_hbm, blocks, table_sem.at[0]),
        pltpu.make_async_copy(probe_hbm, probe, table_sem.at[1]),
    ]
    own_counts = pltpu.make_async_copy(counts_hbm.at[mine], counts, counts_recv.at[0])
    below_slot = lax.rem(me - lax.rem(below, spread) + cuts, cuts)
    below_owns = (lax.rem(below_slot, spread) == 0) & (lax.div(below_slot, spread) >= half)
    next_counts = pltpu.make_async_remote_copy(
        counts_hbm.at[lax.div(below_slot, spread)],
        counts,
        counts_send.at[0],
        counts_recv.at[0],
        **device(below, me),
    )

    for copy in loads + table_loads:
        copy.start()

    barrier = pltpu.get_barrier_semaphore()
    for d in range(1, cuts):
        pl.semaphore_signal(barrier, inc=1, **device(tile, lax.rem(me + d, cuts)))
    pl.semaphore_signal(barrier, inc=1, **device(above, me))
    pl.semaphore_signal(barrier, inc=1, **device(below, me))

    row_at = lax.broadcasted_iota(jnp.int32, (n, n), 0)
    col_at = lax.broadcasted_iota(jnp.int32, (n, n), 1)

    def window(k, target, own):
        row = lax.rem(jnp.where(own, places[0, k], places_before[0, k]), n)
        column = jnp.where(own, places[1, k], places_before[1, k])
        block = lax.div(column, n)
        lower = (row_at >= row).astype(jnp.int32)
        keep = lower == own.astype(jnp.int32)
        wanted = jnp.where(col_at >= column - block * n, block, block + 1)
        for s in range(slices):
            for i, source in enumerate((real, imag)):
                value = jnp.zeros((n, n), f32)
                for at in range(cols // n):
                    value = jnp.where(wanted == at, source[s, :, at * n : (at + 1) * n], value)
                target[k, s, i] = jnp.where(keep, value, 0.0)

    def turn(j, near):
        group = lax.rem(lax.div(j, half) + lax.rem(tile, 2) + (0 if near else 1), 2)
        return group * half + lax.rem(lax.div(me, spread) + j, half)

    def rim_copy(k):
        return pltpu.make_async_remote_copy(
            rim_out.at[k], rim_in.at[k], rim_send.at[k], rim_recv.at[k], **device(jnp.where(k < half, above, below), me)
        )

    def owner(k):
        return lax.rem(k * spread + phase, cuts)

    def gather_copy(k):
        return pltpu.make_async_remote_copy(
            merged.at[k], patches.at[me], gather_send.at[k], gather_recv.at[me], **device(tile, owner(k))
        )

    def arrival(z):
        return pltpu.make_async_remote_copy(
            merged.at[0], patches.at[z], gather_send.at[0], gather_recv.at[z], **device(tile, z)
        )

    for copy in loads:
        copy.wait()
    pl.semaphore_wait(barrier, cuts + 1)

    def send_rim(j, carry):
        k = turn(j, False)
        window(k, rim_out, k >= half)
        rim_copy(k).start()
        return carry

    lax.fori_loop(0, count, send_rim, 0)

    @pl.when(below_owns)
    def _():
        next_counts.start()

    @pl.when(is_owner & (mine < half))
    def _():
        own_counts.start()


    def take_own(j, carry):
        k = turn(j, True)
        window(k, merged, k < half)
        return carry

    lax.fori_loop(0, count, take_own, 0)

    def send_windows(j, carry):
        k = turn(j, True)
        rim_copy(k).wait_recv()
        for s in range(slices):
            for i in range(2):
                merged[k, s, i] = merged[k, s, i] + rim_in[k, s, i]

        @pl.when(owner(k) != me)
        def _():
            gather_copy(k).start()

        @pl.when(owner(k) == me)
        def _():
            for s in range(slices):
                for i in range(2):
                    patches[me, s, i] = merged[k, s, i]

        return carry

    for copy in table_loads:
        copy.wait()

    @pl.when(is_owner)
    def _():
        for i in range(blocks.shape[0]):
            which, other = (i // 2) * 2 + i % 2, (i // 2) * 2 + 1 - i % 2
            high = blocks[i].astype(bf16)
            low, rest = split(blocks[i] - high.astype(f32))
            for j, part in enumerate((high, low, rest)):
                at = slice(j * 2 * n, (j + 1) * 2 * n)
                rights[which, at, :] = part
                lefts[other, :, at] = part

    lax.fori_loop(0, count, send_windows, 0)

    def back_copy(s):
        inner = lax.rem(s, slices)
        return pltpu.make_async_remote_copy(
            contrib.at[s],
            own_out.at[mine, inner],
            back_send.at[s],
            back_recv.at[mine, inner],
            **device(tile, lax.div(s, slices)),
        )

    def keep_copy(s):
        return pltpu.make_async_copy(
            contrib.at[s], own_out.at[mine, lax.rem(s, slices)], back_send.at[s]
        )

    def put(s, re, im):
        a, b = psi[s, 0], psi[s, 1]
        contrib[s, 0] = a * re + b * im
        contrib[s, 1] = a * im - b * re
        z = lax.div(s, slices)

        @pl.when(z != me)
        def _():
            back_copy(s).start()

        @pl.when(z == me)
        def _():
            keep_copy(s).start()

    def patch_at(s):
        z, inner = lax.div(s, slices), lax.rem(s, slices)
        return patches[z, inner, 0], patches[z, inner, 1]

    @pl.when(is_owner)
    def _():
        row = lax.rem(jnp.where(mine < half, places[0, mine], places_before[0, mine]), n)
        column = lax.rem(jnp.where(mine < half, places[1, mine], places_before[1, mine]), n)
        a, b = probe[0], probe[1]
        bit = 1
        while bit < n:
            for axis, amount in ((0, row), (1, column)):
                take = (jnp.full((n, n), amount, jnp.int32) & bit) > 0
                a = jnp.where(take, pltpu.roll(a, bit, axis), a)
                b = jnp.where(take, pltpu.roll(b, bit, axis), b)
            bit *= 2
        psi[0, 0] = a
        psi[0, 1] = b

        def forward(s, carry):
            z = lax.div(s, slices)

            @pl.when((lax.rem(s, slices) == 0) & (z != me))
            def _():
                arrival(z).wait_recv()

            a, b = psi[s, 0], psi[s, 1]
            p, q = patch_at(s)
            re, im = both_sides(p * a - q * b, p * b + q * a, rights, lefts, RIGHT_A)
            psi[s + 1, 0] = re
            psi[s + 1, 1] = im
            return carry

        lax.fori_loop(0, total - 1, forward, 0)
        a, b = psi[total - 1, 0], psi[total - 1, 1]
        p, q = patch_at(total - 1)
        re, im = both_sides(p * a - q * b, p * b + q * a, rights, lefts, RIGHT_F)

        @pl.when(mine < half)
        def _():
            own_counts.wait()

        @pl.when(mine >= half)
        def _():
            next_counts.wait_recv()

        weight = 4.0 * (re * re + im * im - counts[...].astype(f32))
        re, im = both_sides(weight * re, weight * im, rights, lefts, RIGHT_F_CONJ)
        put(total - 1, re, im)

        def backward(i, carry):
            re, im = carry
            s = total - 1 - i
            p, q = patch_at(s)
            re, im = both_sides(p * re + q * im, p * im - q * re, rights, lefts, RIGHT_A_CONJ)
            put(s - 1, re, im)
            return re, im

        lax.fori_loop(0, total - 1, backward, (re, im))

    def term_copy(k, s):
        return pltpu.make_async_remote_copy(
            contrib.at[0], own_out.at[k, s], back_send.at[0], back_recv.at[k, s], **device(tile, owner(k))
        )

    def ahead_copy(k, s):
        return pltpu.make_async_remote_copy(
            own_out.at[k, s], other_out.at[k, s], ahead_send.at[k, s], ahead_recv.at[k, s], **device(jnp.where(k < half, below, above), me)
        )

    def pass_on(step, carry):
        s = slices - 1 - lax.rem(lax.div(step, half), slices)
        k = turn(lax.div(step, half * slices) * half + lax.rem(step, half), False)

        @pl.when(owner(k) != me)
        def _():
            term_copy(k, s).wait_recv()

        @pl.when(owner(k) == me)
        def _():
            keep_copy(me * slices + s).wait()

        ahead_copy(k, s).start()
        return carry

    lax.fori_loop(0, count * slices, pass_on, 0)

    def finish(step, carry):
        s, k = lax.div(step, count), lax.rem(step, count)
        ahead_copy(k, s).wait()
        return carry

    lax.fori_loop(0, count * slices, finish, 0)

    def finish_windows(k, carry):
        rim_copy(k).wait_send()

        @pl.when(owner(k) != me)
        def _():
            gather_copy(k).wait_send()

        return carry

    lax.fori_loop(0, count, finish_windows, 0)

    @pl.when(below_owns)
    def _():
        next_counts.wait_send()


    @pl.when(is_owner)
    def _():
        def finish_back(s, carry):
            @pl.when(lax.div(s, slices) != me)
            def _():
                back_copy(s).wait_send()

            return carry

        lax.fori_loop(0, total, finish_back, 0)


def add_kernel(places, places_before, own, other, real, imag):
    n = own.shape[-1]
    count = own.shape[0]
    rows = lax.broadcasted_iota(jnp.int32, (n, n), 0)
    cols = lax.broadcasted_iota(jnp.int32, (n, n), 1)
    last = real.shape[2] // n - 1
    real[...] = jnp.zeros_like(real)
    imag[...] = jnp.zeros_like(imag)
    for source, first_own in ((own, True), (other, False)):
        for k in range(count):
            is_own = (k < count // 2) == first_own
            where = places if is_own else places_before
            row = lax.rem(where[0, k], n)
            column = where[1, k]
            block = lax.div(column, n)
            keep = (rows >= row) if is_own else (rows < row)
            here = pl.ds(pl.multiple_of(block * n, n), n)
            beside = pl.ds(pl.multiple_of(jnp.minimum(block + 1, last) * n, n), n)
            first = cols >= column - block * n
            for i, target in enumerate((real, imag)):
                value = jnp.where(keep, source[k, 0, i], 0.0)
                target[0, :, here] += jnp.where(first, value, 0.0)
                target[0, :, beside] += jnp.where(first, 0.0, value)


def add(places, places_before, own, other, shape):
    slices, rows, cols = shape
    count, _, _, n, _ = own.shape
    window = pl.BlockSpec((count, 1, 2, n, n), lambda s, *_: (0, s, 0, 0, 0))
    strip = pl.BlockSpec((1, rows, cols), lambda s, *_: (s, 0, 0))
    return pl.pallas_call(
        add_kernel,
        out_shape=(jax.ShapeDtypeStruct(shape, f32),) * 2,
        grid_spec=pltpu.PrefetchScalarGridSpec(
            num_scalar_prefetch=2,
            grid=(slices,),
            in_specs=[window, window],
            out_specs=(strip, strip),
        ),
        compiler_params=pltpu.CompilerParams(vmem_limit_bytes=62 << 20),
    )(places, places_before, own, other)


def shards(object_real, object_imag, probe, positions, counts):
    cuts, tiles = lax.axis_size(CUTS), lax.axis_size(TILE)
    slices, rows, cols = object_real.shape
    n = probe.shape[1]
    count = positions.shape[0]
    positions = positions.T
    before = lax.ppermute(positions, TILE, [(t, (t + 1) % tiles) for t in range(tiles)])
    blocks = jnp.asarray(tables(n))
    windows = (count, slices, 2, n, n)
    total = cuts * slices
    smem = pl.BlockSpec(memory_space=pltpu.SMEM)
    hbm = pl.BlockSpec(memory_space=pltpu.HBM)
    dma = pltpu.SemaphoreType.DMA
    own, other = pl.pallas_call(
        fused_kernel,
        out_shape=(jax.ShapeDtypeStruct(windows, f32),) * 2,
        in_specs=[smem, smem, hbm, hbm, hbm, hbm, hbm],
        out_specs=(hbm, hbm),
        scratch_shapes=[
            pltpu.VMEM(object_real.shape, f32),
            pltpu.VMEM(object_imag.shape, f32),
            pltpu.VMEM(probe.shape, f32),
            pltpu.VMEM((n, n), jnp.int32),
            pltpu.VMEM(blocks.shape, f32),
            pltpu.VMEM((4, 6 * n, 2 * n), bf16),
            pltpu.VMEM((4, 2 * n, 6 * n), bf16),
            pltpu.VMEM(windows, f32),
            pltpu.VMEM(windows, f32),
            pltpu.VMEM(windows, f32),
            pltpu.VMEM((cuts, slices, 2, n, n), f32),
            pltpu.VMEM((total, 2, n, n), f32),
            pltpu.VMEM((total, 2, n, n), f32),
            dma((2, slices)),
            dma((2,)),
            dma((1,)),
            dma((1,)),
            dma((count,)),
            dma((count,)),
            dma((count,)),
            dma((cuts,)),
            dma((total,)),
            dma((count, slices)),
            dma((count, slices)),
            dma((count, slices)),
        ],
        compiler_params=pltpu.CompilerParams(
            collective_id=0, has_side_effects=True, vmem_limit_bytes=62 << 20
        ),
    )(positions, before, probe, counts, object_real, object_imag, blocks)
    return add(positions, before, own, other, object_real.shape)


def solution(mesh):
    placed = (
        P("cuts", "tile", None),
        P("cuts", "tile", None),
        P(),
        P("tile", None),
        P("tile", None, None),
    )
    return jax.shard_map(
        shards,
        mesh=mesh,
        in_specs=placed,
        out_specs=(P("cuts", "tile", None), P("cuts", "tile", None)),
        check_vma=False,
    )
```

```python
import functools
import math

import jax
import jax.numpy as jnp
import numpy as np
from jax import lax
from jax.experimental import pallas as pl
from jax.experimental.pallas import tpu as pltpu
from jax.sharding import PartitionSpec as P

f32, bf16 = jnp.float32, jnp.bfloat16
phase_scale = 32.0
TILE, CUTS = "tile", "cuts"
TURNS = 4
RIGHT_A, RIGHT_A_CONJ, RIGHT_F, RIGHT_F_CONJ = range(4)


def tables(n):
    index = np.arange(n)
    dft = np.exp(-2j * np.pi * (np.outer(index, index) % n) / n) / math.sqrt(n)
    freq = np.where(index < n // 2, index, index - n).astype(np.float64)
    turn = np.exp(-1j * phase_scale * freq**2 / (n * n))
    step = np.conj(dft) @ (turn[:, None] * dft)

    out = []
    for matrix in (step, dft):
        block = np.block([[matrix.real, matrix.imag], [-matrix.imag, matrix.real]])
        out += [block, block.T]
    return np.stack(out).astype(np.float32)


def split(value):
    high = value.astype(bf16)
    return high, (value - high.astype(f32)).astype(bf16)


def dot(a, b):
    return jnp.dot(a, b, preferred_element_type=f32)


def right_times(re, im, table, turn):
    n = re.shape[1]
    high, low = split(jnp.concatenate([re, im], 1))
    main = table[: 2 * n]
    rest = table[pl.ds(pl.multiple_of((turn + 1) * 2 * n, 2 * n), 2 * n), :]
    out = dot(jnp.concatenate([low, high, high], 1), jnp.concatenate([main, main, rest], 0))
    return out[:, :n], out[:, n:]


def left_times(re, im, table, turn):
    n = re.shape[0]
    high, low = split(jnp.concatenate([re, im], 0))
    main = dot(table[:, : 2 * n], jnp.concatenate([high, low], 1))
    rest = dot(table[:, pl.ds(pl.multiple_of((turn + 1) * 2 * n, 2 * n), 2 * n)], high)
    out = main[:, :n] + main[:, n:] + rest
    return out[:n], out[n:]


def both_sides(re, im, rights, lefts, which, turn):
    re, im = right_times(re, im, rights.at[which], turn)
    return left_times(re, im, lefts.at[which], turn)


def fused_kernel(
    places,
    places_before,
    probe_hbm,
    counts_hbm,
    real_hbm,
    imag_hbm,
    blocks_hbm,
    own_out,
    other_out,
    real,
    imag,
    probe,
    counts,
    blocks,
    rights,
    lefts,
    rim_out,
    rim_in,
    merged,
    patches,
    psi,
    contrib,
    load_sem,
    table_sem,
    counts_send,
    counts_recv,
    rim_send,
    rim_recv,
    gather_send,
    gather_recv,
    back_send,
    back_recv,
    ahead_send,
    ahead_recv,
):
    cuts, tiles = lax.axis_size(CUTS), lax.axis_size(TILE)
    me, tile = lax.axis_index(CUTS), lax.axis_index(TILE)
    above = lax.rem(tile + tiles - 1, tiles)
    below = lax.rem(tile + 1, tiles)
    slices, rows, cols = real.shape
    n = probe.shape[1]
    count = merged.shape[0]
    total = cuts * slices
    spread = cuts // count
    phase = lax.rem(tile, spread)
    mine = lax.div(lax.rem(me - phase + cuts, cuts), spread)
    is_owner = lax.rem(me - phase + cuts, spread) == 0
    half = count // 2

    def device(t, z):
        return dict(device_id=(t, z), device_id_type=pl.DeviceIdType.MESH)

    loads = []
    for i, (source, target) in enumerate(((real_hbm, real), (imag_hbm, imag))):
        for s in range(slices):
            loads.append(pltpu.make_async_copy(source.at[s], target.at[s], load_sem.at[i, s]))
    table_loads = [
        pltpu.make_async_copy(blocks_hbm, blocks, table_sem.at[0]),
        pltpu.make_async_copy(probe_hbm, probe, table_sem.at[1]),
    ]
    own_counts = pltpu.make_async_copy(counts_hbm.at[mine], counts, counts_recv.at[0])
    below_slot = lax.rem(me - lax.rem(below, spread) + cuts, cuts)
    below_owns = (lax.rem(below_slot, spread) == 0) & (lax.div(below_slot, spread) >= half)
    next_counts = pltpu.make_async_remote_copy(
        counts_hbm.at[lax.div(below_slot, spread)],
        counts,
        counts_send.at[0],
        counts_recv.at[0],
        **device(below, me),
    )

    for copy in loads + table_loads:
        copy.start()

    barrier = pltpu.get_barrier_semaphore()
    for d in range(1, cuts):
        pl.semaphore_signal(barrier, inc=1, **device(tile, lax.rem(me + d, cuts)))
    pl.semaphore_signal(barrier, inc=1, **device(above, me))
    pl.semaphore_signal(barrier, inc=1, **device(below, me))

    row_at = lax.broadcasted_iota(jnp.int32, (n, n), 0)
    col_at = lax.broadcasted_iota(jnp.int32, (n, n), 1)

    def window(k, target, own):
        row = lax.rem(jnp.where(own, places[0, k], places_before[0, k]), n)
        column = jnp.where(own, places[1, k], places_before[1, k])
        block = lax.div(column, n)
        lower = (row_at >= row).astype(jnp.int32)
        keep = lower == own.astype(jnp.int32)
        wanted = jnp.where(col_at >= column - block * n, block, block + 1)
        for s in range(slices):
            for i, source in enumerate((real, imag)):
                value = jnp.zeros((n, n), f32)
                for at in range(cols // n):
                    value = jnp.where(wanted == at, source[s, :, at * n : (at + 1) * n], value)
                target[k, s, i] = jnp.where(keep, value, 0.0)

    def turn(j, near):
        group = lax.rem(lax.div(j, half) + lax.rem(tile, 2) + (0 if near else 1), 2)
        return group * half + lax.rem(lax.div(me, spread) + j, half)

    def rim_copy(k):
        return pltpu.make_async_remote_copy(
            rim_out.at[k], rim_in.at[k], rim_send.at[k], rim_recv.at[k], **device(jnp.where(k < half, above, below), me)
        )

    def owner(k):
        return lax.rem(k * spread + phase, cuts)

    def gather_copy(k):
        return pltpu.make_async_remote_copy(
            merged.at[k], patches.at[me], gather_send.at[k], gather_recv.at[me], **device(tile, owner(k))
        )

    def arrival(z):
        return pltpu.make_async_remote_copy(
            merged.at[0], patches.at[z], gather_send.at[0], gather_recv.at[z], **device(tile, z)
        )

    for copy in loads:
        copy.wait()
    pl.semaphore_wait(barrier, cuts + 1)

    def send_rim(j, carry):
        k = turn(j, False)
        window(k, rim_out, k >= half)
        rim_copy(k).start()
        return carry

    lax.fori_loop(0, count, send_rim, 0)

    @pl.when(below_owns)
    def _():
        next_counts.start()

    @pl.when(is_owner & (mine < half))
    def _():
        own_counts.start()


    def send_windows(j, carry):
        k = turn(j, True)
        window(k, merged, k < half)
        rim_copy(k).wait_recv()
        for s in range(slices):
            for i in range(2):
                merged[k, s, i] = merged[k, s, i] + rim_in[k, s, i]

        @pl.when(owner(k) != me)
        def _():
            gather_copy(k).start()

        @pl.when(owner(k) == me)
        def _():
            for s in range(slices):
                for i in range(2):
                    patches[me, s, i] = merged[k, s, i]

        return carry

    lax.fori_loop(0, count, send_windows, 0)
    for copy in table_loads:
        copy.wait()

    @pl.when(is_owner)
    def _():
        for i in range(blocks.shape[0]):
            which, other = (i // 2) * 2 + i % 2, (i // 2) * 2 + 1 - i % 2
            high = blocks[i].astype(bf16)
            rest = blocks[i] - high.astype(f32)
            parts, taken = [high], jnp.zeros_like(rest)
            for j in range(TURNS):
                parts.append((rest * (j + 1.0) - taken).astype(bf16))
                taken = taken + parts[-1].astype(f32)
            for j, part in enumerate(parts):
                at = slice(j * 2 * n, (j + 1) * 2 * n)
                rights[which, at, :] = part
                lefts[other, :, at] = part

    def back_copy(s):
        inner = lax.rem(s, slices)
        return pltpu.make_async_remote_copy(
            contrib.at[s],
            own_out.at[mine, inner],
            back_send.at[s],
            back_recv.at[mine, inner],
            **device(tile, lax.div(s, slices)),
        )

    def keep_copy(s):
        return pltpu.make_async_copy(
            contrib.at[s], own_out.at[mine, lax.rem(s, slices)], back_send.at[s]
        )

    def put(s, re, im):
        a, b = psi[s, 0], psi[s, 1]
        contrib[s, 0] = a * re + b * im
        contrib[s, 1] = a * im - b * re

        @pl.when(lax.rem(s, slices) == slices - 1)
        def _():
            send_terms(s)

    def send_terms(s):
        z = lax.div(s, slices)

        @pl.when(z != me)
        def _():
            back_copy(s).start()

        @pl.when(z == me)
        def _():
            keep_copy(s).start()

    def patch_at(s):
        z, inner = lax.div(s, slices), lax.rem(s, slices)
        return patches[z, inner, 0], patches[z, inner, 1]

    @pl.when(is_owner)
    def _():
        row = lax.rem(jnp.where(mine < half, places[0, mine], places_before[0, mine]), n)
        column = lax.rem(jnp.where(mine < half, places[1, mine], places_before[1, mine]), n)
        a, b = probe[0], probe[1]
        bit = 1
        while bit < n:
            for axis, amount in ((0, row), (1, column)):
                take = (jnp.full((n, n), amount, jnp.int32) & bit) > 0
                a = jnp.where(take, pltpu.roll(a, bit, axis), a)
                b = jnp.where(take, pltpu.roll(b, bit, axis), b)
            bit *= 2
        psi[0, 0] = a
        psi[0, 1] = b

        def forward(s, carry):
            z = lax.div(s, slices)

            @pl.when((lax.rem(s, slices) == 0) & (z != me))
            def _():
                arrival(z).wait_recv()

            a, b = psi[s, 0], psi[s, 1]
            p, q = patch_at(s)
            re, im = both_sides(p * a - q * b, p * b + q * a, rights, lefts, RIGHT_A, lax.rem(s, TURNS))
            psi[s + 1, 0] = re
            psi[s + 1, 1] = im
            return carry

        lax.fori_loop(0, total - 1, forward, 0)
        a, b = psi[total - 1, 0], psi[total - 1, 1]
        p, q = patch_at(total - 1)
        re, im = both_sides(p * a - q * b, p * b + q * a, rights, lefts, RIGHT_F, 0)

        @pl.when(mine < half)
        def _():
            own_counts.wait()

        @pl.when(mine >= half)
        def _():
            next_counts.wait_recv()

        weight = 4.0 * (re * re + im * im - counts[...].astype(f32))
        re, im = both_sides(weight * re, weight * im, rights, lefts, RIGHT_F_CONJ, 0)
        put(total - 1, re, im)

        def backward(i, carry):
            re, im = carry
            s = total - 1 - i
            p, q = patch_at(s)
            re, im = both_sides(p * re + q * im, p * im - q * re, rights, lefts, RIGHT_A_CONJ, lax.rem(i, TURNS))
            put(s - 1, re, im)
            return re, im

        lax.fori_loop(0, total - 1, backward, (re, im))

        def send_rest(step, carry):
            inner = slices - 2 - lax.div(step, cuts)
            send_terms(lax.rem(me + cuts // 2 + step, cuts) * slices + inner)
            return carry

        lax.fori_loop(0, cuts * (slices - 1), send_rest, 0)

    def term_copy(k, s):
        return pltpu.make_async_remote_copy(
            contrib.at[0], own_out.at[k, s], back_send.at[0], back_recv.at[k, s], **device(tile, owner(k))
        )

    def ahead_copy(k, s):
        return pltpu.make_async_remote_copy(
            own_out.at[k, s], other_out.at[k, s], ahead_send.at[k, s], ahead_recv.at[k, s], **device(jnp.where(k < half, below, above), me)
        )

    def pass_on(step, carry):
        s = slices - 1 - lax.div(step, count)
        k = turn(lax.rem(step, count), False)

        @pl.when(owner(k) != me)
        def _():
            term_copy(k, s).wait_recv()

        @pl.when(owner(k) == me)
        def _():
            keep_copy(me * slices + s).wait()

        ahead_copy(k, s).start()
        return carry

    lax.fori_loop(0, count * slices, pass_on, 0)

    def finish(step, carry):
        s, k = lax.div(step, count), lax.rem(step, count)
        ahead_copy(k, s).wait()
        return carry

    lax.fori_loop(0, count * slices, finish, 0)

    def finish_windows(k, carry):
        rim_copy(k).wait_send()

        @pl.when(owner(k) != me)
        def _():
            gather_copy(k).wait_send()

        return carry

    lax.fori_loop(0, count, finish_windows, 0)

    @pl.when(below_owns)
    def _():
        next_counts.wait_send()


    @pl.when(is_owner)
    def _():
        def finish_back(s, carry):
            @pl.when(lax.div(s, slices) != me)
            def _():
                back_copy(s).wait_send()

            return carry

        lax.fori_loop(0, total, finish_back, 0)


def add_kernel(places, places_before, own_hbm, other_hbm, real_hbm, imag_hbm, own, other, strip, load_sem, store_sem):
    count, slices, _, n, _ = own.shape
    last = strip.shape[3] // n - 1
    loads = []
    for s in range(slices):
        for i, (source, target) in enumerate(((own_hbm, own), (other_hbm, other))):
            copy = pltpu.make_async_copy(source.at[:, s], target.at[:, s], load_sem.at[s, i])
            copy.start()
            loads.append(copy)
    strip[...] = jnp.zeros_like(strip)
    rows = lax.broadcasted_iota(jnp.int32, (n, n), 0)
    cols = lax.broadcasted_iota(jnp.int32, (n, n), 1)
    stores = []
    for s in range(slices):
        loads[2 * s].wait()
        loads[2 * s + 1].wait()
        for i, target in enumerate((real_hbm, imag_hbm)):
            for source, first_own in ((own, True), (other, False)):
                for k in range(count):
                    is_own = (k < count // 2) == first_own
                    where = places if is_own else places_before
                    row = lax.rem(where[0, k], n)
                    column = where[1, k]
                    block = lax.div(column, n)
                    keep = (rows >= row) if is_own else (rows < row)
                    here = pl.ds(pl.multiple_of(block * n, n), n)
                    beside = pl.ds(pl.multiple_of(jnp.minimum(block + 1, last) * n, n), n)
                    first = cols >= column - block * n
                    value = jnp.where(keep, source[k, s, i], 0.0)
                    strip[s, i, :, here] += jnp.where(first, value, 0.0)
                    strip[s, i, :, beside] += jnp.where(first, 0.0, value)
            copy = pltpu.make_async_copy(strip.at[s, i], target.at[s], store_sem.at[s, i])
            copy.start()
            stores.append(copy)
    for copy in stores:
        copy.wait()


def add(places, places_before, own, other, shape):
    slices, rows, cols = shape
    smem = pl.BlockSpec(memory_space=pltpu.SMEM)
    hbm = pl.BlockSpec(memory_space=pltpu.HBM)
    return pl.pallas_call(
        add_kernel,
        out_shape=(jax.ShapeDtypeStruct(shape, f32),) * 2,
        in_specs=[smem, smem, hbm, hbm],
        out_specs=(hbm, hbm),
        scratch_shapes=[
            pltpu.VMEM(own.shape, f32),
            pltpu.VMEM(other.shape, f32),
            pltpu.VMEM((slices, 2, rows, cols), f32),
            pltpu.SemaphoreType.DMA((slices, 2)),
            pltpu.SemaphoreType.DMA((slices, 2)),
        ],
        compiler_params=pltpu.CompilerParams(vmem_limit_bytes=62 << 20),
    )(places, places_before, own, other)


def shards(object_real, object_imag, probe, positions, counts):
    cuts, tiles = lax.axis_size(CUTS), lax.axis_size(TILE)
    slices, rows, cols = object_real.shape
    n = probe.shape[1]
    count = positions.shape[0]
    positions = positions.T
    before = lax.ppermute(positions, TILE, [(t, (t + 1) % tiles) for t in range(tiles)])
    blocks = jnp.asarray(tables(n))
    windows = (count, slices, 2, n, n)
    total = cuts * slices
    smem = pl.BlockSpec(memory_space=pltpu.SMEM)
    hbm = pl.BlockSpec(memory_space=pltpu.HBM)
    dma = pltpu.SemaphoreType.DMA
    own, other = pl.pallas_call(
        fused_kernel,
        out_shape=(jax.ShapeDtypeStruct(windows, f32),) * 2,
        in_specs=[smem, smem, hbm, hbm, hbm, hbm, hbm],
        out_specs=(hbm, hbm),
        scratch_shapes=[
            pltpu.VMEM(object_real.shape, f32),
            pltpu.VMEM(object_imag.shape, f32),
            pltpu.VMEM(probe.shape, f32),
            pltpu.VMEM((n, n), jnp.int32),
            pltpu.VMEM(blocks.shape, f32),
            pltpu.VMEM((4, (TURNS + 1) * 2 * n, 2 * n), bf16),
            pltpu.VMEM((4, 2 * n, (TURNS + 1) * 2 * n), bf16),
            pltpu.VMEM(windows, f32),
            pltpu.VMEM(windows, f32),
            pltpu.VMEM(windows, f32),
            pltpu.VMEM((cuts, slices, 2, n, n), f32),
            pltpu.VMEM((total, 2, n, n), f32),
            pltpu.VMEM((total, 2, n, n), f32),
            dma((2, slices)),
            dma((2,)),
            dma((1,)),
            dma((1,)),
            dma((count,)),
            dma((count,)),
            dma((count,)),
            dma((cuts,)),
            dma((total,)),
            dma((count, slices)),
            dma((count, slices)),
            dma((count, slices)),
        ],
        compiler_params=pltpu.CompilerParams(
            collective_id=0, has_side_effects=True, vmem_limit_bytes=62 << 20
        ),
    )(positions, before, probe, counts, object_real, object_imag, blocks)
    return add(positions, before, own, other, object_real.shape)


def solution(mesh):
    placed = (
        P("cuts", "tile", None),
        P("cuts", "tile", None),
        P(),
        P("tile", None),
        P("tile", None, None),
    )
    return jax.shard_map(
        shards,
        mesh=mesh,
        in_specs=placed,
        out_specs=(P("cuts", "tile", None), P("cuts", "tile", None)),
        check_vma=False,
    )
```

```python
import functools
import math

import jax
import jax.numpy as jnp
import numpy as np
from jax import lax
from jax.experimental import pallas as pl
from jax.experimental.pallas import tpu as pltpu
from jax.sharding import PartitionSpec as P

f32, bf16 = jnp.float32, jnp.bfloat16
phase_scale = 32.0
TILE, CUTS = "tile", "cuts"
TURNS = 4
RIGHT_A, RIGHT_A_CONJ, RIGHT_F, RIGHT_F_CONJ = range(4)


def tables(n):
    index = np.arange(n)
    dft = np.exp(-2j * np.pi * (np.outer(index, index) % n) / n) / math.sqrt(n)
    freq = np.where(index < n // 2, index, index - n).astype(np.float64)
    turn = np.exp(-1j * phase_scale * freq**2 / (n * n))
    step = np.conj(dft) @ (turn[:, None] * dft)

    out = []
    for matrix in (step, dft):
        block = np.block([[matrix.real, matrix.imag], [-matrix.imag, matrix.real]])
        out += [block, block.T]
    return np.stack(out).astype(np.float32)


def split(value):
    high = value.astype(bf16)
    return high, (value - high.astype(f32)).astype(bf16)


def dot(a, b):
    return jnp.dot(a, b, preferred_element_type=f32)


def right_times(re, im, table, turn):
    n = re.shape[1]
    high, low = split(jnp.concatenate([re, im], 1))
    main = table[: 2 * n]
    rest = table[pl.ds(pl.multiple_of((turn + 1) * 2 * n, 2 * n), 2 * n), :]
    out = dot(jnp.concatenate([low, high, high], 1), jnp.concatenate([main, main, rest], 0))
    return out[:, :n], out[:, n:]


def left_times(re, im, table, turn):
    n = re.shape[0]
    high, low = split(jnp.concatenate([re, im], 0))
    main = dot(table[:, : 2 * n], jnp.concatenate([high, low], 1))
    rest = dot(table[:, pl.ds(pl.multiple_of((turn + 1) * 2 * n, 2 * n), 2 * n)], high)
    out = main[:, :n] + main[:, n:] + rest
    return out[:n], out[n:]


def both_sides(re, im, rights, lefts, which, turn):
    re, im = right_times(re, im, rights.at[which], turn)
    return left_times(re, im, lefts.at[which], turn)


def fused_kernel(
    places,
    places_before,
    probe_hbm,
    counts_hbm,
    real_hbm,
    imag_hbm,
    blocks_hbm,
    own_out,
    other_out,
    real,
    imag,
    probe,
    counts,
    blocks,
    rights,
    lefts,
    rim_out,
    rim_in,
    merged,
    patches,
    psi,
    contrib,
    load_sem,
    table_sem,
    counts_send,
    counts_recv,
    rim_send,
    rim_recv,
    gather_send,
    gather_recv,
    back_send,
    back_recv,
    ahead_send,
    ahead_recv,
):
    cuts, tiles = lax.axis_size(CUTS), lax.axis_size(TILE)
    me, tile = lax.axis_index(CUTS), lax.axis_index(TILE)
    above = lax.rem(tile + tiles - 1, tiles)
    below = lax.rem(tile + 1, tiles)
    slices, rows, cols = real.shape
    n = probe.shape[1]
    count = merged.shape[0]
    total = cuts * slices
    spread = cuts // count
    phase = lax.rem(tile, spread)
    mine = lax.div(lax.rem(me - phase + cuts, cuts), spread)
    is_owner = lax.rem(me - phase + cuts, spread) == 0
    half = count // 2

    def device(t, z):
        return dict(device_id=(t, z), device_id_type=pl.DeviceIdType.MESH)

    loads = []
    for i, (source, target) in enumerate(((real_hbm, real), (imag_hbm, imag))):
        for s in range(slices):
            loads.append(pltpu.make_async_copy(source.at[s], target.at[s], load_sem.at[i, s]))
    table_loads = [
        pltpu.make_async_copy(blocks_hbm, blocks, table_sem.at[0]),
        pltpu.make_async_copy(probe_hbm, probe, table_sem.at[1]),
    ]
    own_counts = pltpu.make_async_copy(counts_hbm.at[mine], counts, counts_recv.at[0])
    below_slot = lax.rem(me - lax.rem(below, spread) + cuts, cuts)
    below_owns = (lax.rem(below_slot, spread) == 0) & (lax.div(below_slot, spread) >= half)
    next_counts = pltpu.make_async_remote_copy(
        counts_hbm.at[lax.div(below_slot, spread)],
        counts,
        counts_send.at[0],
        counts_recv.at[0],
        **device(below, me),
    )

    for copy in loads + table_loads:
        copy.start()

    barrier = pltpu.get_barrier_semaphore()
    for d in range(1, cuts):
        pl.semaphore_signal(barrier, inc=1, **device(tile, lax.rem(me + d, cuts)))
    pl.semaphore_signal(barrier, inc=1, **device(above, me))
    pl.semaphore_signal(barrier, inc=1, **device(below, me))

    row_at = lax.broadcasted_iota(jnp.int32, (n, n), 0)
    col_at = lax.broadcasted_iota(jnp.int32, (n, n), 1)

    def window(k, target, own):
        row = lax.rem(jnp.where(own, places[0, k], places_before[0, k]), n)
        column = jnp.where(own, places[1, k], places_before[1, k])
        block = lax.div(column, n)
        lower = (row_at >= row).astype(jnp.int32)
        keep = lower == own.astype(jnp.int32)
        wanted = jnp.where(col_at >= column - block * n, block, block + 1)
        for s in range(slices):
            for i, source in enumerate((real, imag)):
                value = jnp.zeros((n, n), f32)
                for at in range(cols // n):
                    value = jnp.where(wanted == at, source[s, :, at * n : (at + 1) * n], value)
                target[k, s, i] = jnp.where(keep, value, 0.0)

    def turn(j, near):
        group = lax.rem(lax.div(j, half) + lax.rem(tile, 2) + (0 if near else 1), 2)
        return group * half + lax.rem(lax.div(me, spread) + j, half)

    def rim_copy(k):
        return pltpu.make_async_remote_copy(
            rim_out.at[k], rim_in.at[k], rim_send.at[k], rim_recv.at[k], **device(jnp.where(k < half, above, below), me)
        )

    def owner(k):
        return lax.rem(k * spread + phase, cuts)

    def gather_copy(k, s):
        return pltpu.make_async_remote_copy(
            merged.at[k, s], patches.at[me, s], gather_send.at[k, s], gather_recv.at[me, s], **device(tile, owner(k))
        )

    def arrival(z, s):
        return pltpu.make_async_remote_copy(
            merged.at[0, s], patches.at[z, s], gather_send.at[0, s], gather_recv.at[z, s], **device(tile, z)
        )

    for copy in loads:
        copy.wait()
    pl.semaphore_wait(barrier, cuts + 1)

    def send_rim(j, carry):
        k = turn(j, False)
        window(k, rim_out, k >= half)
        rim_copy(k).start()
        return carry

    lax.fori_loop(0, count, send_rim, 0)

    @pl.when(below_owns)
    def _():
        next_counts.start()

    @pl.when(is_owner & (mine < half))
    def _():
        own_counts.start()


    def send_windows(j, carry):
        k = turn(j, True)
        window(k, merged, k < half)
        rim_copy(k).wait_recv()
        for s in range(slices):
            for i in range(2):
                merged[k, s, i] = merged[k, s, i] + rim_in[k, s, i]

        @pl.when(owner(k) != me)
        def _():
            for s in range(slices):
                gather_copy(k, s).start()

        @pl.when(owner(k) == me)
        def _():
            for s in range(slices):
                for i in range(2):
                    patches[me, s, i] = merged[k, s, i]

        return carry

    lax.fori_loop(0, count, send_windows, 0)
    for copy in table_loads:
        copy.wait()

    @pl.when(is_owner)
    def _():
        for i in range(blocks.shape[0]):
            which, other = (i // 2) * 2 + i % 2, (i // 2) * 2 + 1 - i % 2
            high = blocks[i].astype(bf16)
            rest = blocks[i] - high.astype(f32)
            parts, taken = [high], jnp.zeros_like(rest)
            for j in range(TURNS):
                parts.append((rest * (j + 1.0) - taken).astype(bf16))
                taken = taken + parts[-1].astype(f32)
            for j, part in enumerate(parts):
                at = slice(j * 2 * n, (j + 1) * 2 * n)
                rights[which, at, :] = part
                lefts[other, :, at] = part

    def back_copy(s):
        inner = lax.rem(s, slices)
        return pltpu.make_async_remote_copy(
            contrib.at[s],
            own_out.at[mine, inner],
            back_send.at[s],
            back_recv.at[mine, inner],
            **device(tile, lax.div(s, slices)),
        )

    def keep_copy(s):
        return pltpu.make_async_copy(
            contrib.at[s], own_out.at[mine, lax.rem(s, slices)], back_send.at[s]
        )

    def put(s, re, im):
        a, b = psi[s, 0], psi[s, 1]
        contrib[s, 0] = a * re + b * im
        contrib[s, 1] = a * im - b * re

        @pl.when(lax.rem(s, slices) == slices - 1)
        def _():
            send_terms(s)

    def send_terms(s):
        z = lax.div(s, slices)

        @pl.when(z != me)
        def _():
            back_copy(s).start()

        @pl.when(z == me)
        def _():
            keep_copy(s).start()

    def patch_at(s):
        z, inner = lax.div(s, slices), lax.rem(s, slices)
        return patches[z, inner, 0], patches[z, inner, 1]

    @pl.when(is_owner)
    def _():
        row = lax.rem(jnp.where(mine < half, places[0, mine], places_before[0, mine]), n)
        column = lax.rem(jnp.where(mine < half, places[1, mine], places_before[1, mine]), n)
        a, b = probe[0], probe[1]
        bit = 1
        while bit < n:
            for axis, amount in ((0, row), (1, column)):
                take = (jnp.full((n, n), amount, jnp.int32) & bit) > 0
                a = jnp.where(take, pltpu.roll(a, bit, axis), a)
                b = jnp.where(take, pltpu.roll(b, bit, axis), b)
            bit *= 2
        psi[0, 0] = a
        psi[0, 1] = b

        def forward(s, carry):
            z = lax.div(s, slices)

            @pl.when(z != me)
            def _():
                arrival(z, lax.rem(s, slices)).wait_recv()

            a, b = psi[s, 0], psi[s, 1]
            p, q = patch_at(s)
            re, im = both_sides(p * a - q * b, p * b + q * a, rights, lefts, RIGHT_A, lax.rem(s, TURNS))
            psi[s + 1, 0] = re
            psi[s + 1, 1] = im
            return carry

        lax.fori_loop(0, total - 1, forward, 0)

        @pl.when(me != cuts - 1)
        def _():
            arrival(cuts - 1, slices - 1).wait_recv()

        a, b = psi[total - 1, 0], psi[total - 1, 1]
        p, q = patch_at(total - 1)
        re, im = both_sides(p * a - q * b, p * b + q * a, rights, lefts, RIGHT_F, 0)

        @pl.when(mine < half)
        def _():
            own_counts.wait()

        @pl.when(mine >= half)
        def _():
            next_counts.wait_recv()

        weight = 4.0 * (re * re + im * im - counts[...].astype(f32))
        re, im = both_sides(weight * re, weight * im, rights, lefts, RIGHT_F_CONJ, 0)
        put(total - 1, re, im)

        def backward(i, carry):
            re, im = carry
            s = total - 1 - i
            p, q = patch_at(s)
            re, im = both_sides(p * re + q * im, p * im - q * re, rights, lefts, RIGHT_A_CONJ, lax.rem(i, TURNS))
            put(s - 1, re, im)
            return re, im

        lax.fori_loop(0, total - 1, backward, (re, im))

        def send_rest(step, carry):
            inner = slices - 2 - lax.div(step, cuts)
            send_terms(lax.rem(me + cuts // 2 + step, cuts) * slices + inner)
            return carry

        lax.fori_loop(0, cuts * (slices - 1), send_rest, 0)

    def term_copy(k, s):
        return pltpu.make_async_remote_copy(
            contrib.at[0], own_out.at[k, s], back_send.at[0], back_recv.at[k, s], **device(tile, owner(k))
        )

    def ahead_copy(k, s):
        return pltpu.make_async_remote_copy(
            own_out.at[k, s], other_out.at[k, s], ahead_send.at[k, s], ahead_recv.at[k, s], **device(jnp.where(k < half, below, above), me)
        )

    def pass_on(step, carry):
        s = slices - 1 - lax.div(step, count)
        k = turn(lax.rem(step, count), False)

        @pl.when(owner(k) != me)
        def _():
            term_copy(k, s).wait_recv()

        @pl.when(owner(k) == me)
        def _():
            keep_copy(me * slices + s).wait()

        ahead_copy(k, s).start()
        return carry

    lax.fori_loop(0, count * slices, pass_on, 0)

    def finish(step, carry):
        s, k = lax.div(step, count), lax.rem(step, count)
        ahead_copy(k, s).wait()
        return carry

    lax.fori_loop(0, count * slices, finish, 0)

    def finish_windows(k, carry):
        rim_copy(k).wait_send()

        @pl.when(owner(k) != me)
        def _():
            for s in range(slices):
                gather_copy(k, s).wait_send()

        return carry

    lax.fori_loop(0, count, finish_windows, 0)

    @pl.when(below_owns)
    def _():
        next_counts.wait_send()


    @pl.when(is_owner)
    def _():
        def finish_back(s, carry):
            @pl.when(lax.div(s, slices) != me)
            def _():
                back_copy(s).wait_send()

            return carry

        lax.fori_loop(0, total, finish_back, 0)


def add_kernel(places, places_before, own_hbm, other_hbm, real_hbm, imag_hbm, own, other, strip, load_sem, store_sem):
    count, slices, _, n, _ = own.shape
    last = strip.shape[3] // n - 1
    loads = []
    for s in range(slices):
        for i, (source, target) in enumerate(((own_hbm, own), (other_hbm, other))):
            copy = pltpu.make_async_copy(source.at[:, s], target.at[:, s], load_sem.at[s, i])
            copy.start()
            loads.append(copy)
    strip[...] = jnp.zeros_like(strip)
    rows = lax.broadcasted_iota(jnp.int32, (n, n), 0)
    cols = lax.broadcasted_iota(jnp.int32, (n, n), 1)
    stores = []
    for s in range(slices):
        loads[2 * s].wait()
        loads[2 * s + 1].wait()
        for i, target in enumerate((real_hbm, imag_hbm)):
            for source, first_own in ((own, True), (other, False)):
                for k in range(count):
                    is_own = (k < count // 2) == first_own
                    where = places if is_own else places_before
                    row = lax.rem(where[0, k], n)
                    column = where[1, k]
                    block = lax.div(column, n)
                    keep = (rows >= row) if is_own else (rows < row)
                    here = pl.ds(pl.multiple_of(block * n, n), n)
                    beside = pl.ds(pl.multiple_of(jnp.minimum(block + 1, last) * n, n), n)
                    first = cols >= column - block * n
                    value = jnp.where(keep, source[k, s, i], 0.0)
                    strip[s, i, :, here] += jnp.where(first, value, 0.0)
                    strip[s, i, :, beside] += jnp.where(first, 0.0, value)
            copy = pltpu.make_async_copy(strip.at[s, i], target.at[s], store_sem.at[s, i])
            copy.start()
            stores.append(copy)
    for copy in stores:
        copy.wait()


def add(places, places_before, own, other, shape):
    slices, rows, cols = shape
    smem = pl.BlockSpec(memory_space=pltpu.SMEM)
    hbm = pl.BlockSpec(memory_space=pltpu.HBM)
    return pl.pallas_call(
        add_kernel,
        out_shape=(jax.ShapeDtypeStruct(shape, f32),) * 2,
        in_specs=[smem, smem, hbm, hbm],
        out_specs=(hbm, hbm),
        scratch_shapes=[
            pltpu.VMEM(own.shape, f32),
            pltpu.VMEM(other.shape, f32),
            pltpu.VMEM((slices, 2, rows, cols), f32),
            pltpu.SemaphoreType.DMA((slices, 2)),
            pltpu.SemaphoreType.DMA((slices, 2)),
        ],
        compiler_params=pltpu.CompilerParams(vmem_limit_bytes=62 << 20),
    )(places, places_before, own, other)


def shards(object_real, object_imag, probe, positions, counts):
    cuts, tiles = lax.axis_size(CUTS), lax.axis_size(TILE)
    slices, rows, cols = object_real.shape
    n = probe.shape[1]
    count = positions.shape[0]
    positions = positions.T
    before = lax.ppermute(positions, TILE, [(t, (t + 1) % tiles) for t in range(tiles)])
    blocks = jnp.asarray(tables(n))
    windows = (count, slices, 2, n, n)
    total = cuts * slices
    smem = pl.BlockSpec(memory_space=pltpu.SMEM)
    hbm = pl.BlockSpec(memory_space=pltpu.HBM)
    dma = pltpu.SemaphoreType.DMA
    own, other = pl.pallas_call(
        fused_kernel,
        out_shape=(jax.ShapeDtypeStruct(windows, f32),) * 2,
        in_specs=[smem, smem, hbm, hbm, hbm, hbm, hbm],
        out_specs=(hbm, hbm),
        scratch_shapes=[
            pltpu.VMEM(object_real.shape, f32),
            pltpu.VMEM(object_imag.shape, f32),
            pltpu.VMEM(probe.shape, f32),
            pltpu.VMEM((n, n), jnp.int32),
            pltpu.VMEM(blocks.shape, f32),
            pltpu.VMEM((4, (TURNS + 1) * 2 * n, 2 * n), bf16),
            pltpu.VMEM((4, 2 * n, (TURNS + 1) * 2 * n), bf16),
            pltpu.VMEM(windows, f32),
            pltpu.VMEM(windows, f32),
            pltpu.VMEM(windows, f32),
            pltpu.VMEM((cuts, slices, 2, n, n), f32),
            pltpu.VMEM((total, 2, n, n), f32),
            pltpu.VMEM((total, 2, n, n), f32),
            dma((2, slices)),
            dma((2,)),
            dma((1,)),
            dma((1,)),
            dma((count,)),
            dma((count,)),
            dma((count, slices)),
            dma((cuts, slices)),
            dma((total,)),
            dma((count, slices)),
            dma((count, slices)),
            dma((count, slices)),
        ],
        compiler_params=pltpu.CompilerParams(
            collective_id=0, has_side_effects=True, vmem_limit_bytes=62 << 20
        ),
    )(positions, before, probe, counts, object_real, object_imag, blocks)
    return add(positions, before, own, other, object_real.shape)


def solution(mesh):
    placed = (
        P("cuts", "tile", None),
        P("cuts", "tile", None),
        P(),
        P("tile", None),
        P("tile", None, None),
    )
    return jax.shard_map(
        shards,
        mesh=mesh,
        in_specs=placed,
        out_specs=(P("cuts", "tile", None), P("cuts", "tile", None)),
        check_vma=False,
    )
```
